512 devices in a mesh: row: 32 (over z, core), col: 16 (over y, x).
Axes of the slice: x: 4, y: 4, z: 16, core: 2. Of those that a mesh axis runs over, the one named last changes fastest.
Arguments:
- density: float32 [384, 13, 128, 128], P('row', None, 'col'), may hold values from -1.5 to 1.5
- pattern: int32 [384, 13], P('row'), may hold values from 0 to 1, as said below
Outputs:
- purified: float32 [384, 13, 128, 128], P('row', None, 'col')
The draws below stay inside these ranges and needn't reach their ends.
Inputs may be any that keep to these rules, and one draw needn't show every extreme that they name: `pattern`: each block row has exactly 7 ones, placed at random slots.
All inputs are finite; a program needn't handle non-finite values.
Results may differ from the reference program's by a relative error of at most 0.0003.
Values sent between devices are 32-bit elements; how exact they have to be, the bound alone decides.
No kernel may reach another device: no remote copies, remote signals or barrier semaphores. Data moves between devices by JAX's collectives and lax.ppermute only.
A program may use at most 64 MiB of HBM per device.

```python
import jax
import jax.numpy as jnp
from jax import lax

B = 128
K = 13
NZ = 7
NBLK = 384


def one_order(row_key):
    return jax.random.permutation(row_key, K)


def draw_pattern(key, part):
    key = jax.random.fold_in(key, 7)
    row_keys = jax.random.split(key, NBLK)
    orders = jax.vmap(one_order)(row_keys)
    return (orders < NZ).astype(jnp.int32)


def shard_levels(stream_key, shape, cuts, least, high):
    def one(axis_at, blocks):
        steps = jax.random.uniform(jax.random.fold_in(jax.random.fold_in(stream_key, 6), axis_at), (blocks,), jnp.float32, least / len(cuts), high / len(cuts))
        return jnp.repeat(jnp.exp(steps), shape[axis_at] // blocks).reshape((-1,) + (1,) * (len(shape) - axis_at - 1))

    level = one(*cuts[0])
    for cut in cuts[1:]:
        level = level * one(*cut)
    return level


def noise(rng, shape, spread, reach, shards=(), held_as=jnp.bfloat16):
    entries = jax.random.normal(rng, shape, jnp.float32) * spread
    if len(shards) > 0:
        entries = shard_levels(rng, shape, shards, -0.22, 0.18) * entries
    return jnp.clip(entries, min=-reach, max=reach).astype(held_as)


def setup_inputs(seed: int = 0) -> dict:
    keys = jax.random.split(jax.random.key(seed), 3)
    density = noise(keys[0], (NBLK, K, B, B), 0.1, 1.5, ((0, 32), (2, 16)), jnp.float32)
    pattern = draw_pattern(jax.random.fold_in(keys[2], 71), 0)
    return dict(density=density, pattern=pattern)


def reference(density, pattern):
    total_rows, band_slots, block_size, _ = density.shape
    half_band = (band_slots - 1) // 2
    span_slots = 2 * band_slots - 1
    masked = jnp.swapaxes(density * pattern[:, :, None, None].astype(jnp.float32), 2, 3)
    slot_range = jnp.arange(band_slots, dtype=jnp.int32)
    slot_place = ((slot_range[:, None] + slot_range[None, :])[:, :, None] == jnp.arange(span_slots, dtype=jnp.int32)[None, None, :]).astype(jnp.float32)
    columns = 2 * half_band - slot_range[:, None] + slot_range[None, :]

    def square_row(row_index):
        near_rows = (row_index + slot_range - half_band) % total_rows
        products = jnp.einsum('sac,sdcb->sdab', masked[row_index], masked[near_rows], precision=lax.Precision.HIGHEST)
        return jnp.einsum('sdab,sde->eab', products, slot_place, precision=lax.Precision.HIGHEST)

    square = lax.map(square_row, jnp.arange(total_rows, dtype=jnp.int32))

    def cube_row(row_index):
        near_rows = (row_index + slot_range - half_band) % total_rows
        right_blocks = square[near_rows[:, None], columns]
        return jnp.einsum('sac,sicb->iab', masked[row_index], right_blocks, precision=lax.Precision.HIGHEST)

    third_power = lax.map(cube_row, jnp.arange(total_rows, dtype=jnp.int32))
    band_core = square[:, half_band:half_band + band_slots]
    result = (3.0 * band_core - 2.0 * third_power) * pattern[:, :, None, None].astype(jnp.float32)
    return jnp.swapaxes(result, 2, 3)
```

```python
import functools

import jax
import jax.numpy as jnp
from jax import lax
from jax.experimental import pallas as pl
from jax.experimental.pallas import tpu as pltpu
from jax.sharding import PartitionSpec as P

HALF = 6
SLOTS = 13
ONES = 7
COLS = 8
B = 128
CHUNK = HALF * ONES
PAIRS = HALF // 2
VIEW = 14 * COLS
WIDE = 26 * COLS
HALO = 18 * COLS
DEPTH = 14 * B
NEAR = (-1, 1, 2)
F32 = jnp.float32
BF16 = jnp.bfloat16
AXES = ("row", "col")


def flipped(core, index, last):
    return jnp.where(core == 0, index, last - index)


def split(value):
    high = value.astype(BF16)
    return high, (value - high.astype(F32)).astype(BF16)


def prepare(pattern, density, packed, dense0, dense1, slots):
    core = lax.rem(lax.axis_index("row"), 2)
    for chunk, dense in enumerate((dense0, dense1)):

        @pl.loop(0, HALF)
        def _(v):
            u = chunk * HALF + v
            r = flipped(core, u, 2 * HALF - 1)
            rank = jnp.int32(0)
            for s in range(SLOTS):
                place = flipped(core, s, SLOTS - 1)
                on = pattern[r, place]
                dense[v, s] = density[r, place] * on.astype(F32)
                slots[rank] = place
                rank = rank + on
            for t in range(ONES):
                packed[u * ONES + t] = density[r, slots[t]]


def paired(first, second):
    gap = jnp.zeros((COLS, B), F32)
    return jnp.concatenate(
        [jnp.concatenate([first, gap], axis=0), jnp.concatenate([gap, second], axis=0)], axis=1
    )


def square_kernel(chunk, pattern, own, a1m, a1p, a1o, a2m, a2p, a2o, far_m, far_p, far_o, before, middle, after,
                  square, halo, w_high_out, w_low_out, raw, w_high, w_low, sides, slots, raw_sems, out_sems):
    core = lax.rem(lax.axis_index("row"), 2)
    col = lax.axis_index("col")
    y, x = col // 4, lax.rem(col, 4)

    def place(step1, step2):
        down = jnp.where(core == 0, step2, step1)
        over = jnp.where(core == 0, step1, step2)
        return pl.multiple_of(((y + down + 4) % 4 * 4 + (x + over + 4) % 4) * COLS, COLS)

    first = chunk * CHUNK
    sources = [(own.at[pl.ds(first, CHUNK)], 0, 0)]
    for ref, step in zip((a1m, a1p, a1o), NEAR):
        sources.append((ref.at[pl.ds(first, CHUNK)], step, 0))
    for ref, step in zip((a2m, a2p, a2o), NEAR):
        sources.append((ref.at[pl.ds(first, CHUNK)], 0, step))
    for ref, step in zip((far_m, far_p, far_o), NEAR):
        for i, other in enumerate(NEAR):
            sources.append((ref.at[pl.ds(i * CHUNK, CHUNK)], other, step))
    copies = []
    for i, (ref, step1, step2) in enumerate(sources):
        copies.append(
            pltpu.make_async_copy(ref, raw.at[:, pl.ds(place(step1, step2), COLS), :], raw_sems.at[i])
        )
        copies[-1].start()

    def other_way(ref, v):
        return jnp.concatenate([ref[HALF - 1 - v, SLOTS - 1 - s] for s in range(SLOTS)], axis=0)

    def same_way(ref, v):
        return jnp.concatenate([ref[v, s] for s in range(SLOTS)], axis=0)

    for part, ref in enumerate((before, middle, after)):
        turned = part == (0 if chunk == 0 else 2)
        take = other_way if turned else same_way
        for i in range(PAIRS):
            high, low = split(paired(take(ref, 2 * i), take(ref, 2 * i + 1)))
            sides[part * PAIRS + i, :VIEW] = high
            sides[part * PAIRS + i, VIEW:] = low

    for i in range(PAIRS):
        w_high[i] = jnp.zeros((DEPTH, 2 * B), BF16)
        w_low[i] = jnp.zeros((DEPTH, 2 * B), BF16)
    for v in range(HALF):
        r = flipped(core, chunk * HALF + v, 2 * HALF - 1)
        rank = jnp.int32(0)
        for s in range(SLOTS):
            slots[v * 8 + rank] = s
            rank = rank + pattern[r, flipped(core, s, SLOTS - 1)]
    for copy in copies:
        copy.wait()
    outs = []
    for i in range(PAIRS):
        for q in range(2):
            v = 2 * i + q
            for t in range(ONES):
                high, low = split(raw[v * ONES + t])
                rows = pl.ds(pl.multiple_of((slots[v * 8 + t] + q) * B, B), B)
                w_high[i, rows, q * B : (q + 1) * B] = high
                w_low[i, rows, q * B : (q + 1) * B] = low
        for k, (here, there) in enumerate(((w_high, w_high_out), (w_low, w_low_out))):
            outs.append(pltpu.make_async_copy(here.at[i], there.at[i], out_sems.at[2 * i + k]))
            outs[-1].start()

    for i in range(PAIRS):
        square[i] = jnp.zeros((WIDE, 2 * B), F32)
        for m in range(7):
            depth = slice(m * 2 * B, (m + 1) * 2 * B)
            whole = jnp.dot(sides[i + m], w_high[i, depth], preferred_element_type=F32)
            small = jnp.dot(sides[i + m, :VIEW], w_low[i, depth], preferred_element_type=F32)
            square[i, 2 * COLS * m : 2 * COLS * m + VIEW] += whole[:VIEW] + whole[VIEW:] + small
        if chunk == 0:
            halo[i] = square[i, :HALO]
        else:
            halo[i] = square[i, WIDE - HALO :]
    for copy in outs:
        copy.wait()


def lift(ref, held):
    for i in range(PAIRS):
        held[0, i], held[1, i] = split(ref[i])


def lift_halo(ref, held, first):
    for i in range(PAIRS):
        source = ref[PAIRS - 1 - i]
        turned = jnp.concatenate(
            [source[(HALO // COLS - 1 - j) * COLS : (HALO // COLS - j) * COLS] for j in range(HALO // COLS)], axis=0
        )
        turned = jnp.concatenate([turned[:, B:], turned[:, :B]], axis=1)
        held[0, i, first : first + HALO], held[1, i, first : first + HALO] = split(turned)


def add_products(total, held, part, w_high, w_low):
    for i in range(PAIRS):
        value = None
        for k in range(PAIRS):
            m = part * PAIRS + k - i
            if m < 0 or m > 6:
                continue
            rows = slice(2 * COLS * (6 - m), 2 * COLS * (6 - m) + VIEW)
            depth = slice(m * 2 * B, (m + 1) * 2 * B)
            high, low = held[0, k, rows], held[1, k, rows]
            term = (
                jnp.dot(high, w_high[i, depth], preferred_element_type=F32)
                + jnp.dot(low, w_high[i, depth], preferred_element_type=F32)
                + jnp.dot(high, w_low[i, depth], preferred_element_type=F32)
            )
            value = term if value is None else value + term
        total[i] += value


def third_first(halo, square0, w_high, w_low, total, held_halo, held):
    total[...] = jnp.zeros_like(total)
    lift(square0, held)
    lift_halo(halo, held_halo, WIDE - HALO)
    add_products(total, held, 1, w_high, w_low)
    add_products(total, held_halo, 0, w_high, w_low)


def third_second(square0, square1, w_high0, w_low0, w_high1, w_low1, before, total0, total1, held0, held1):
    lift(square0, held0)
    lift(square1, held1)
    total0[...] = before[...]
    total1[...] = jnp.zeros_like(total1)
    add_products(total0, held1, 2, w_high0, w_low0)
    add_products(total1, held0, 0, w_high1, w_low1)
    add_products(total1, held1, 1, w_high1, w_low1)


def finish(pattern, halo, square0, square1, w_high1, w_low1, total0, before1, out, total1, held):
    core = lax.rem(lax.axis_index("row"), 2)
    lift_halo(halo, held, 0)
    total1[...] = before1[...]
    add_products(total1, held, 2, w_high1, w_low1)
    for chunk, (square, total) in enumerate(((square0, total0), (square1, total1))):
        for i in range(PAIRS):
            value = 3.0 * square[i, 6 * COLS : 6 * COLS + VIEW] - 2.0 * total[i]
            for q in range(2):
                r = flipped(core, chunk * HALF + 2 * i + q, 2 * HALF - 1)
                for s in range(SLOTS):
                    place = flipped(core, s, SLOTS - 1)
                    tile = value[(s + q) * COLS : (s + q + 1) * COLS, q * B : (q + 1) * B]
                    out[r, place] = tile * pattern[r, place].astype(F32)


ANY = pl.BlockSpec(memory_space=pl.ANY)
VMEM = pl.BlockSpec(memory_space=pltpu.VMEM)
SMEM = pl.BlockSpec(memory_space=pltpu.SMEM)
PARAMS = pltpu.CompilerParams(vmem_limit_bytes=48 * 1024 * 1024)


def cost(products):
    flops = 2 * products * 3 * VIEW * 256 * 256
    return pl.CostEstimate(flops=flops, bytes_accessed=4_000_000, transcendentals=0)


def shape(*dims, dtype=F32):
    return jax.ShapeDtypeStruct(dims, dtype)


def shards(density, pattern):
    spots = [(z, c, y, x) for z in range(16) for c in range(2) for y in range(4) for x in range(4)]

    def number(z, c, y, x):
        return (z % 16 * 2 + c) * 16 + y % 4 * 4 + x % 4

    def send(value, move):
        return lax.ppermute(value, AXES, [(number(*spot), number(*move(*spot))) for spot in spots])

    def first_way(step):
        return lambda z, c, y, x: (z, c, y, x + step) if c == 0 else (z, c, y + step, x)

    def second_way(step):
        return lambda z, c, y, x: (z, c, y + step, x) if c == 0 else (z, c, y, x + step)

    def next_chip(z, c, y, x):
        return (z - 1, 1, y, x) if c == 0 else (z + 1, 0, y, x)

    def other_core(z, c, y, x):
        return (z, 1 - c, y, x)

    packed, dense0, dense1 = pl.pallas_call(
        prepare,
        out_shape=(shape(2 * CHUNK, COLS, B), shape(HALF, SLOTS, COLS, B), shape(HALF, SLOTS, COLS, B)),
        in_specs=[SMEM, VMEM],
        out_specs=(VMEM, VMEM, VMEM),
        scratch_shapes=[pltpu.SMEM((8,), jnp.int32)],
        compiler_params=PARAMS,
        name="prepare",
    )(pattern, density)

    steps = (1, -1, 2)
    along1 = [send(packed, first_way(step)) for step in steps]
    along2 = [send(packed, second_way(step)) for step in steps]
    halo_z = send(dense0, next_chip)
    halo_c = send(dense1, other_core)
    far = []
    for chunk in range(2):
        three = jnp.concatenate([piece[chunk * CHUNK : (chunk + 1) * CHUNK] for piece in along1])
        far.append([send(three, second_way(step)) for step in steps])

    weights = shape(PAIRS, DEPTH, 2 * B, dtype=BF16)

    def squared(chunk, before, middle, after):
        return pl.pallas_call(
            functools.partial(square_kernel, chunk),
            out_shape=(shape(PAIRS, WIDE, 2 * B), shape(PAIRS, HALO, 2 * B), weights, weights),
            in_specs=[SMEM] + [ANY] * 10 + [VMEM] * 3,
            out_specs=(VMEM, VMEM, ANY, ANY),
            scratch_shapes=[
                pltpu.VMEM((CHUNK, B, B), F32),
                pltpu.VMEM((PAIRS, DEPTH, 2 * B), BF16),
                pltpu.VMEM((PAIRS, DEPTH, 2 * B), BF16),
                pltpu.VMEM((3 * PAIRS, 2 * VIEW, 2 * B), BF16),
                pltpu.SMEM((HALF * 8,), jnp.int32),
                pltpu.SemaphoreType.DMA((16,)),
                pltpu.SemaphoreType.DMA((2 * PAIRS,)),
            ],
            compiler_params=PARAMS,
            cost_estimate=cost(21),
            name=f"square{chunk}",
        )(pattern, packed, *along1, *along2, *far[chunk], before, middle, after)

    square0, edge0, w_high0, w_low0 = squared(0, halo_z, dense0, dense1)
    square_z = send(edge0, next_chip)
    totals = shape(PAIRS, VIEW, 2 * B)
    held = pltpu.VMEM((2, PAIRS, WIDE, 2 * B), BF16)
    total0 = pl.pallas_call(
        third_first,
        out_shape=totals,
        in_specs=[VMEM] * 4,
        out_specs=VMEM,
        scratch_shapes=[held, held],
        compiler_params=PARAMS,
        cost_estimate=cost(15),
        name="third_first",
    )(square_z, square0, w_high0, w_low0)
    square1, edge1, w_high1, w_low1 = squared(1, dense0, dense1, halo_c)
    square_c = send(edge1, other_core)
    total0, total1 = pl.pallas_call(
        third_second,
        out_shape=(totals, totals),
        in_specs=[VMEM] * 7,
        out_specs=(VMEM, VMEM),
        scratch_shapes=[held, held],
        compiler_params=PARAMS,
        cost_estimate=cost(21),
        name="third_second",
    )(square0, square1, w_high0, w_low0, w_high1, w_low1, total0)
    return pl.pallas_call(
        finish,
        out_shape=shape(2 * HALF, SLOTS, COLS, B),
        in_specs=[SMEM] + [VMEM] * 7,
        out_specs=VMEM,
        scratch_shapes=[pltpu.VMEM((PAIRS, VIEW, 2 * B), F32), held],
        compiler_params=PARAMS,
        cost_estimate=cost(6),
        name="finish",
    )(pattern, square_c, square0, square1, w_high1, w_low1, total0, total1)


def solution(mesh):
    placed = (P("row", None, "col", None), P("row", None))
    return jax.shard_map(
        shards, mesh=mesh, in_specs=placed, out_specs=P("row", None, "col", None), check_vma=False
    )
```

```python
import functools

import jax
import jax.numpy as jnp
from jax import lax
from jax.experimental import pallas as pl
from jax.experimental.pallas import tpu as pltpu
from jax.sharding import PartitionSpec as P

HALF = 6
SLOTS = 13
ONES = 7
COLS = 8
B = 128
CHUNK = HALF * ONES
PAIRS = HALF // 2
VIEW = 14 * COLS
WIDE = 26 * COLS
HALO = 18 * COLS
DEPTH = 14 * B
F32 = jnp.float32
BF16 = jnp.bfloat16
AXES = ("row", "col")


def flipped(core, index, last):
    return jnp.where(core == 0, index, last - index)


def split(value):
    high = value.astype(BF16)
    return high, (value - high.astype(F32)).astype(BF16)


def prepare(pattern, density, packed, dense0, dense1, slots):
    core = lax.rem(lax.axis_index("row"), 2)
    for chunk, dense in enumerate((dense0, dense1)):

        @pl.loop(0, HALF)
        def _(v):
            u = chunk * HALF + v
            r = flipped(core, u, 2 * HALF - 1)
            rank = jnp.int32(0)
            for s in range(SLOTS):
                place = flipped(core, s, SLOTS - 1)
                on = pattern[r, place]
                dense[v, s] = density[r, place] * on.astype(F32)
                slots[rank] = place
                rank = rank + on
            for t in range(ONES):
                tile = density[r, slots[t]]
                for copy in range(4):
                    packed[copy, u * ONES + t] = tile


def paired(first, second):
    gap = jnp.zeros((COLS, B), F32)
    return jnp.concatenate(
        [jnp.concatenate([first, gap], axis=0), jnp.concatenate([gap, second], axis=0)], axis=1
    )


def square_kernel(chunk, pattern, near, far_m, far_p, far_o, before, middle, after,
                  square, halo, w_high, w_low, raw, sides, slots):
    core = lax.rem(lax.axis_index("row"), 2)
    col = lax.axis_index("col")
    y, x = col // 4, lax.rem(col, 4)

    second = jnp.where(core == 0, y, x)
    for ref, base, step in ((near, chunk * CHUNK, 0), (far_m, 0, -1), (far_p, 0, 1), (far_o, 0, 2)):
        other = lax.rem(second + step + 4, 4)
        for i in range(4):
            spot = jnp.where(core == 0, other * 4 + i, i * 4 + other)
            rows = pl.ds(pl.multiple_of(spot * COLS, COLS), COLS)
            for t in range(CHUNK):
                raw[t, rows, :] = ref[i, base + t]

    def other_way(ref, v):
        return jnp.concatenate([ref[HALF - 1 - v, SLOTS - 1 - s] for s in range(SLOTS)], axis=0)

    def same_way(ref, v):
        return jnp.concatenate([ref[v, s] for s in range(SLOTS)], axis=0)

    for part, ref in enumerate((before, middle, after)):
        turned = part == (0 if chunk == 0 else 2)
        take = other_way if turned else same_way
        for i in range(PAIRS):
            high, low = split(paired(take(ref, 2 * i), take(ref, 2 * i + 1)))
            sides[part * PAIRS + i, :VIEW] = high
            sides[part * PAIRS + i, VIEW:] = low

    for i in range(PAIRS):
        w_high[i] = jnp.zeros((DEPTH, 2 * B), BF16)
        w_low[i] = jnp.zeros((DEPTH, 2 * B), BF16)
    for v in range(HALF):
        r = flipped(core, chunk * HALF + v, 2 * HALF - 1)
        rank = jnp.int32(0)
        for s in range(SLOTS):
            slots[v * 8 + rank] = s
            rank = rank + pattern[r, flipped(core, s, SLOTS - 1)]
    for i in range(PAIRS):
        for q in range(2):
            v = 2 * i + q
            for t in range(ONES):
                high, low = split(raw[v * ONES + t])
                rows = pl.ds(pl.multiple_of((slots[v * 8 + t] + q) * B, B), B)
                w_high[i, rows, q * B : (q + 1) * B] = high
                w_low[i, rows, q * B : (q + 1) * B] = low

    for i in range(PAIRS):
        square[i] = jnp.zeros((WIDE, 2 * B), F32)
        for m in range(7):
            depth = slice(m * 2 * B, (m + 1) * 2 * B)
            whole = jnp.dot(sides[i + m], w_high[i, depth], preferred_element_type=F32)
            small = jnp.dot(sides[i + m, :VIEW], w_low[i, depth], preferred_element_type=F32)
            square[i, 2 * COLS * m : 2 * COLS * m + VIEW] += whole[:VIEW] + whole[VIEW:] + small
        if chunk == 0:
            halo[i] = square[i, :HALO]
        else:
            halo[i] = square[i, WIDE - HALO :]


def lift(ref, held):
    for i in range(PAIRS):
        held[0, i], held[1, i] = split(ref[i])


def lift_halo(ref, held, first):
    for i in range(PAIRS):
        source = ref[PAIRS - 1 - i]
        turned = jnp.concatenate(
            [source[(HALO // COLS - 1 - j) * COLS : (HALO // COLS - j) * COLS] for j in range(HALO // COLS)], axis=0
        )
        turned = jnp.concatenate([turned[:, B:], turned[:, :B]], axis=1)
        held[0, i, first : first + HALO], held[1, i, first : first + HALO] = split(turned)


def add_products(total, held, part, w_high, w_low):
    for i in range(PAIRS):
        value = None
        for k in range(PAIRS):
            m = part * PAIRS + k - i
            if m < 0 or m > 6:
                continue
            rows = slice(2 * COLS * (6 - m), 2 * COLS * (6 - m) + VIEW)
            depth = slice(m * 2 * B, (m + 1) * 2 * B)
            high, low = held[0, k, rows], held[1, k, rows]
            term = (
                jnp.dot(high, w_high[i, depth], preferred_element_type=F32)
                + jnp.dot(low, w_high[i, depth], preferred_element_type=F32)
                + jnp.dot(high, w_low[i, depth], preferred_element_type=F32)
            )
            value = term if value is None else value + term
        total[i] += value


def third_first(halo, square0, w_high, w_low, total, held_halo, held):
    total[...] = jnp.zeros_like(total)
    lift(square0, held)
    lift_halo(halo, held_halo, WIDE - HALO)
    add_products(total, held, 1, w_high, w_low)
    add_products(total, held_halo, 0, w_high, w_low)


def third_second(square0, square1, w_high0, w_low0, w_high1, w_low1, before, total0, total1, held0, held1):
    lift(square0, held0)
    lift(square1, held1)
    total0[...] = before[...]
    total1[...] = jnp.zeros_like(total1)
    add_products(total0, held1, 2, w_high0, w_low0)
    add_products(total1, held0, 0, w_high1, w_low1)
    add_products(total1, held1, 1, w_high1, w_low1)


def finish(pattern, halo, square0, square1, w_high1, w_low1, total0, before1, out, total1, held):
    core = lax.rem(lax.axis_index("row"), 2)
    lift_halo(halo, held, 0)
    total1[...] = before1[...]
    add_products(total1, held, 2, w_high1, w_low1)
    for chunk, (square, total) in enumerate(((square0, total0), (square1, total1))):
        for i in range(PAIRS):
            value = 3.0 * square[i, 6 * COLS : 6 * COLS + VIEW] - 2.0 * total[i]
            for q in range(2):
                r = flipped(core, chunk * HALF + 2 * i + q, 2 * HALF - 1)
                for s in range(SLOTS):
                    place = flipped(core, s, SLOTS - 1)
                    tile = value[(s + q) * COLS : (s + q + 1) * COLS, q * B : (q + 1) * B]
                    out[r, place] = tile * pattern[r, place].astype(F32)


VMEM = pl.BlockSpec(memory_space=pltpu.VMEM)
SMEM = pl.BlockSpec(memory_space=pltpu.SMEM)
PARAMS = pltpu.CompilerParams(vmem_limit_bytes=16 * 1024 * 1024)


def cost(products):
    flops = 2 * products * 3 * VIEW * 256 * 256
    return pl.CostEstimate(flops=flops, bytes_accessed=4_000_000, transcendentals=0)


def shape(*dims, dtype=F32):
    return jax.ShapeDtypeStruct(dims, dtype)


def shards(density, pattern):
    spots = [(z, c, y, x) for z in range(16) for c in range(2) for y in range(4) for x in range(4)]

    def number(z, c, y, x):
        return (z % 16 * 2 + c) * 16 + y % 4 * 4 + x % 4

    def send(value, move):
        return lax.ppermute(value, AXES, [(number(*spot), number(*move(*spot))) for spot in spots])

    def second_way(step):
        return lambda z, c, y, x: (z, c, y + step, x) if c == 0 else (z, c, y, x + step)

    def next_chip(z, c, y, x):
        return (z - 1, 1, y, x) if c == 0 else (z + 1, 0, y, x)

    def other_core(z, c, y, x):
        return (z, 1 - c, y, x)

    packed, dense0, dense1 = pl.pallas_call(
        prepare,
        out_shape=(shape(4, 2 * CHUNK, COLS, B), shape(HALF, SLOTS, COLS, B), shape(HALF, SLOTS, COLS, B)),
        in_specs=[SMEM, VMEM],
        out_specs=(VMEM, VMEM, VMEM),
        scratch_shapes=[pltpu.SMEM((8,), jnp.int32)],
        compiler_params=PARAMS,
        name="prepare",
    )(pattern, density)

    quads = []
    for z in range(16):
        for i in range(4):
            quads.append([number(z, 0, i, x) for x in range(4)])
            quads.append([number(z, 1, y, i) for y in range(4)])
    near = lax.all_to_all(packed, AXES, 0, 0, axis_index_groups=quads)
    far = []
    for chunk in range(2):
        part = near[:, chunk * CHUNK : (chunk + 1) * CHUNK]
        far.append([send(part, second_way(step)) for step in (1, -1, 2)])
    halo_z = send(dense0, next_chip)
    halo_c = send(dense1, other_core)

    weights = shape(PAIRS, DEPTH, 2 * B, dtype=BF16)

    def squared(chunk, before, middle, after):
        return pl.pallas_call(
            functools.partial(square_kernel, chunk),
            out_shape=(shape(PAIRS, WIDE, 2 * B), shape(PAIRS, HALO, 2 * B), weights, weights),
            in_specs=[SMEM] + [VMEM] * 7,
            out_specs=(VMEM, VMEM, VMEM, VMEM),
            scratch_shapes=[
                pltpu.VMEM((CHUNK, B, B), F32),
                pltpu.VMEM((3 * PAIRS, 2 * VIEW, 2 * B), BF16),
                pltpu.SMEM((HALF * 8,), jnp.int32),
            ],
            compiler_params=PARAMS,
            cost_estimate=cost(21),
            name=f"square{chunk}",
        )(pattern, near, *far[chunk], before, middle, after)

    square0, edge0, w_high0, w_low0 = squared(0, halo_z, dense0, dense1)
    square_z = send(edge0, next_chip)
    totals = shape(PAIRS, VIEW, 2 * B)
    held = pltpu.VMEM((2, PAIRS, WIDE, 2 * B), BF16)
    total0 = pl.pallas_call(
        third_first,
        out_shape=totals,
        in_specs=[VMEM] * 4,
        out_specs=VMEM,
        scratch_shapes=[held, held],
        compiler_params=PARAMS,
        cost_estimate=cost(15),
        name="third_first",
    )(square_z, square0, w_high0, w_low0)
    total0, halo_c = lax.optimization_barrier((total0, halo_c))
    square1, edge1, w_high1, w_low1 = squared(1, dense0, dense1, halo_c)
    square_c = send(edge1, other_core)
    total0, total1 = pl.pallas_call(
        third_second,
        out_shape=(totals, totals),
        in_specs=[VMEM] * 7,
        out_specs=(VMEM, VMEM),
        scratch_shapes=[held, held],
        compiler_params=PARAMS,
        cost_estimate=cost(21),
        name="third_second",
    )(square0, square1, w_high0, w_low0, w_high1, w_low1, total0)
    return pl.pallas_call(
        finish,
        out_shape=shape(2 * HALF, SLOTS, COLS, B),
        in_specs=[SMEM] + [VMEM] * 7,
        out_specs=VMEM,
        scratch_shapes=[pltpu.VMEM((PAIRS, VIEW, 2 * B), F32), held],
        compiler_params=PARAMS,
        cost_estimate=cost(6),
        name="finish",
    )(pattern, square_c, square0, square1, w_high1, w_low1, total0, total1)


def solution(mesh):
    placed = (P("row", None, "col", None), P("row", None))
    return jax.shard_map(
        shards, mesh=mesh, in_specs=placed, out_specs=P("row", None, "col", None), check_vma=False
    )
```

```python
import functools

import jax
import jax.numpy as jnp
from jax import lax
from jax.experimental import pallas as pl
from jax.experimental.pallas import tpu as pltpu
from jax.sharding import PartitionSpec as P

HALF = 6
SLOTS = 13
ONES = 7
COLS = 8
B = 128
CHUNK = HALF * ONES
PAIRS = HALF // 2
VIEW = 14 * COLS
WIDE = 26 * COLS
HALO = 18 * COLS
DEPTH = 14 * B
F32 = jnp.float32
BF16 = jnp.bfloat16
AXES = ("row", "col")


def flipped(core, index, last):
    return jnp.where(core == 0, index, last - index)


def split(value):
    high = value.astype(BF16)
    return high, (value - high.astype(F32)).astype(BF16)


def row_codes(core, pattern):
    lane = lax.broadcasted_iota(jnp.int32, pattern.shape, 1)
    rank = jnp.zeros(pattern.shape, jnp.int32)
    for s in range(SLOTS - 1):
        rank = rank + jnp.where(lane > s, pattern[:, s : s + 1], 0)
    slot = flipped(core, lane, SLOTS - 1)
    rank = flipped(core, rank, ONES - 1)
    return jnp.sum(pattern * lax.shift_left(slot, 4 * rank), axis=1, keepdims=True)


def code_of(codes, core, row):
    return codes[flipped(core, row, 2 * HALF - 1), 0]


def slot_of(code, t):
    return lax.shift_right_logical(code, 4 * t) & 15


def unused_slots(code):
    held = jnp.int32(0)
    for t in range(ONES):
        held = held | lax.shift_left(jnp.int32(1), slot_of(code, t))
    rest, rank = jnp.int32(0), jnp.int32(0)
    for s in range(SLOTS):
        off = 1 - (lax.shift_right_logical(held, s) & 1)
        rest = rest | (off * lax.shift_left(jnp.int32(s), 4 * rank))
        rank = rank + off
    return rest


def prepare(pattern, density, packed, dense0, dense1, codes):
    core = lax.rem(lax.axis_index("row"), 2)
    codes[...] = jnp.broadcast_to(row_codes(core, pattern[...]), codes.shape)
    for u in range(2 * HALF):
        r = flipped(core, u, 2 * HALF - 1)
        code = codes[r, 0]
        dense = (dense0, dense1)[u // HALF]
        for s in range(SLOTS):
            dense[u % HALF, s] = jnp.zeros((COLS, B), F32)
        for t in range(ONES):
            s = slot_of(code, t)
            tile = density[r, flipped(core, s, SLOTS - 1)]
            dense[u % HALF, s] = tile
            for copy in range(4):
                packed[copy, u * ONES + t] = tile


def paired(first, second):
    gap = jnp.zeros((COLS, B), F32)
    return jnp.concatenate(
        [jnp.concatenate([first, gap], axis=0), jnp.concatenate([gap, second], axis=0)], axis=1
    )


def right_operand(chunk, before, middle, after, sides):
    def other_way(ref, v):
        return jnp.concatenate([ref[HALF - 1 - v, SLOTS - 1 - s] for s in range(SLOTS)], axis=0)

    def same_way(ref, v):
        return jnp.concatenate([ref[v, s] for s in range(SLOTS)], axis=0)

    for part, ref in enumerate((before, middle, after)):
        turned = part == (0 if chunk == 0 else 2)
        take = other_way if turned else same_way
        for i in range(PAIRS):
            high, low = split(paired(take(ref, 2 * i), take(ref, 2 * i + 1)))
            sides[part * PAIRS + i, :VIEW] = high
            sides[part * PAIRS + i, VIEW:] = low


def left_operand(chunk, codes, near, far_m, far_p, far_o, w_high, w_low, raw):
    core = lax.rem(lax.axis_index("row"), 2)
    col = lax.axis_index("col")
    y, x = col // 4, lax.rem(col, 4)

    second = jnp.where(core == 0, y, x)
    for ref, base, step in ((near, chunk * CHUNK, 0), (far_m, 0, -1), (far_p, 0, 1), (far_o, 0, 2)):
        other = lax.rem(second + step + 4, 4)
        for i in range(4):
            spot = jnp.where(core == 0, other * 4 + i, i * 4 + other)
            rows = pl.ds(pl.multiple_of(spot * COLS, COLS), COLS)
            for t in range(CHUNK):
                raw[t, rows, :] = ref[i, base + t]

    nothing = jnp.zeros((B, B), BF16)
    for i in range(PAIRS):
        for q in range(2):
            v = 2 * i + q
            code = code_of(codes, core, chunk * HALF + v)
            rest = unused_slots(code)
            lanes = slice(q * B, (q + 1) * B)
            corner = slice((DEPTH - B) * (1 - q), (DEPTH - B) * (1 - q) + B)
            w_high[i, corner, lanes] = nothing
            w_low[i, corner, lanes] = nothing
            for t in range(SLOTS - ONES):
                rows = pl.ds(pl.multiple_of((slot_of(rest, t) + q) * B, B), B)
                w_high[i, rows, lanes] = nothing
                w_low[i, rows, lanes] = nothing
            for t in range(ONES):
                high, low = split(raw[v * ONES + t])
                rows = pl.ds(pl.multiple_of((slot_of(code, t) + q) * B, B), B)
                w_high[i, rows, lanes] = high
                w_low[i, rows, lanes] = low


def squares(chunk, sides, w_high, w_low, square, halo):
    for i in range(PAIRS):
        square[i] = jnp.zeros((WIDE, 2 * B), F32)
        for m in range(7):
            depth = slice(m * 2 * B, (m + 1) * 2 * B)
            whole = jnp.dot(sides[i + m], w_high[i, depth], preferred_element_type=F32)
            small = jnp.dot(sides[i + m, :VIEW], w_low[i, depth], preferred_element_type=F32)
            square[i, 2 * COLS * m : 2 * COLS * m + VIEW] += whole[:VIEW] + whole[VIEW:] + small
        if chunk == 0:
            halo[i] = square[i, :HALO]
        else:
            halo[i] = square[i, WIDE - HALO :]


def square_kernel(chunk, codes, near, far_m, far_p, far_o, before, middle, after,
                  square, halo, w_high, w_low, raw, sides):
    right_operand(chunk, before, middle, after, sides)
    left_operand(chunk, codes, near, far_m, far_p, far_o, w_high, w_low, raw)
    squares(chunk, sides, w_high, w_low, square, halo)


def lift(ref, held):
    for i in range(PAIRS):
        held[0, i], held[1, i] = split(ref[i])


def lift_halo(ref, held, first):
    for i in range(PAIRS):
        source = ref[PAIRS - 1 - i]
        turned = jnp.concatenate(
            [source[(HALO // COLS - 1 - j) * COLS : (HALO // COLS - j) * COLS] for j in range(HALO // COLS)], axis=0
        )
        turned = jnp.concatenate([turned[:, B:], turned[:, :B]], axis=1)
        held[0, i, first : first + HALO], held[1, i, first : first + HALO] = split(turned)


def add_products(total, held, part, w_high, w_low):
    for i in range(PAIRS):
        value = None
        for k in range(PAIRS):
            m = part * PAIRS + k - i
            if m < 0 or m > 6:
                continue
            rows = slice(2 * COLS * (6 - m), 2 * COLS * (6 - m) + VIEW)
            depth = slice(m * 2 * B, (m + 1) * 2 * B)
            high, low = held[0, k, rows], held[1, k, rows]
            term = (
                jnp.dot(high, w_high[i, depth], preferred_element_type=F32)
                + jnp.dot(low, w_high[i, depth], preferred_element_type=F32)
                + jnp.dot(high, w_low[i, depth], preferred_element_type=F32)
            )
            value = term if value is None else value + term
        total[i] += value


def third_inner(square0, w_high0, w_low0, total0, held0):
    lift(square0, held0)
    total0[...] = jnp.zeros_like(total0)
    add_products(total0, held0, 1, w_high0, w_low0)


def third_second(held0, square1, w_high0, w_low0, w_high1, w_low1, before, total0, total1, held1):
    lift(square1, held1)
    total0[...] = before[...]
    total1[...] = jnp.zeros_like(total1)
    add_products(total0, held1, 2, w_high0, w_low0)
    add_products(total1, held0, 0, w_high1, w_low1)
    add_products(total1, held1, 1, w_high1, w_low1)


def third_outer(halo, w_high0, w_low0, before, total0, held):
    total0[...] = before[...]
    lift_halo(halo, held, WIDE - HALO)
    add_products(total0, held, 0, w_high0, w_low0)


def finish(codes, halo, square0, square1, w_high1, w_low1, total0, before1, out, total1, held):
    core = lax.rem(lax.axis_index("row"), 2)
    lift_halo(halo, held, 0)
    total1[...] = before1[...]
    add_products(total1, held, 2, w_high1, w_low1)
    for chunk, (square, total) in enumerate(((square0, total0), (square1, total1))):
        for i in range(PAIRS):
            value = 3.0 * square[i, 6 * COLS : 6 * COLS + VIEW] - 2.0 * total[i]
            for q in range(2):
                r = flipped(core, chunk * HALF + 2 * i + q, 2 * HALF - 1)
                rest = unused_slots(codes[r, 0])
                for s in range(SLOTS):
                    out[r, flipped(core, s, SLOTS - 1)] = value[(s + q) * COLS : (s + q + 1) * COLS, q * B : (q + 1) * B]
                for t in range(SLOTS - ONES):
                    out[r, flipped(core, slot_of(rest, t), SLOTS - 1)] = jnp.zeros((COLS, B), F32)


VMEM = pl.BlockSpec(memory_space=pltpu.VMEM)
PARAMS = pltpu.CompilerParams(vmem_limit_bytes=16 * 1024 * 1024)


def cost(products):
    flops = 2 * products * 3 * VIEW * 256 * 256
    return pl.CostEstimate(flops=flops, bytes_accessed=4_000_000, transcendentals=0)


def shape(*dims, dtype=F32):
    return jax.ShapeDtypeStruct(dims, dtype)


def shards(density, pattern):
    spots = [(z, c, y, x) for z in range(16) for c in range(2) for y in range(4) for x in range(4)]

    def number(z, c, y, x):
        return (z % 16 * 2 + c) * 16 + y % 4 * 4 + x % 4

    def send(value, move):
        return lax.ppermute(value, AXES, [(number(*spot), number(*move(*spot))) for spot in spots])

    def second_way(step):
        return lambda z, c, y, x: (z, c, y + step, x) if c == 0 else (z, c, y, x + step)

    def next_chip(z, c, y, x):
        return (z - 1, 1, y, x) if c == 0 else (z + 1, 0, y, x)

    def other_core(z, c, y, x):
        return (z, 1 - c, y, x)

    dense_shape = shape(HALF, SLOTS, COLS, B)
    packed, dense0, dense1, codes = pl.pallas_call(
        prepare,
        out_shape=(shape(4, 2 * CHUNK, COLS, B), dense_shape, dense_shape, shape(2 * HALF, B, dtype=jnp.int32)),
        in_specs=[VMEM, VMEM],
        out_specs=(VMEM,) * 4,
        compiler_params=PARAMS,
        name="prepare",
    )(pattern, density)

    quads = []
    for z in range(16):
        for i in range(4):
            quads.append([number(z, 0, i, x) for x in range(4)])
            quads.append([number(z, 1, y, i) for y in range(4)])
    near = lax.all_to_all(packed, AXES, 0, 0, axis_index_groups=quads)
    far = []
    for chunk in range(2):
        part = near[:, chunk * CHUNK : (chunk + 1) * CHUNK]
        far.append([send(part, second_way(step)) for step in (1, -1, 2)])
    halo_z = send(dense0, next_chip)
    weights = shape(PAIRS, DEPTH, 2 * B, dtype=BF16)

    def squared(chunk, *sides):
        return pl.pallas_call(
            functools.partial(square_kernel, chunk),
            out_shape=(shape(PAIRS, WIDE, 2 * B), shape(PAIRS, HALO, 2 * B), weights, weights),
            in_specs=[VMEM] * 8,
            out_specs=(VMEM,) * 4,
            scratch_shapes=[pltpu.VMEM((CHUNK, B, B), F32), pltpu.VMEM((3 * PAIRS, 2 * VIEW, 2 * B), BF16)],
            compiler_params=PARAMS,
            cost_estimate=cost(21),
            name=f"square{chunk}",
        )(codes, near, *far[chunk], *sides)

    square0, edge0, w_high0, w_low0 = squared(0, halo_z, dense0, dense1)
    square_z = send(edge0, next_chip)
    totals = shape(PAIRS, VIEW, 2 * B)
    held_shape = (2, PAIRS, WIDE, 2 * B)
    held = pltpu.VMEM(held_shape, BF16)
    total0, held0 = pl.pallas_call(
        third_inner,
        out_shape=(totals, shape(*held_shape, dtype=BF16)),
        in_specs=[VMEM] * 3,
        out_specs=(VMEM, VMEM),
        compiler_params=PARAMS,
        cost_estimate=cost(9),
        name="third_inner",
    )(square0, w_high0, w_low0)
    dense1_later, far[1][2] = lax.optimization_barrier((dense1, far[1][2]))
    halo_c = send(dense1_later, other_core)
    halo_c, held0 = lax.optimization_barrier((halo_c, held0))
    square1, edge1, w_high1, w_low1 = squared(1, dense0, dense1, halo_c)
    square_c = send(edge1, other_core)
    total0, total1 = pl.pallas_call(
        third_second,
        out_shape=(totals, totals),
        in_specs=[VMEM] * 7,
        out_specs=(VMEM, VMEM),
        scratch_shapes=[held],
        compiler_params=PARAMS,
        cost_estimate=cost(21),
        name="third_second",
    )(held0, square1, w_high0, w_low0, w_high1, w_low1, total0)
    square_z, total0 = lax.optimization_barrier((square_z, total0))
    total0 = pl.pallas_call(
        third_outer,
        out_shape=totals,
        in_specs=[VMEM] * 4,
        out_specs=VMEM,
        scratch_shapes=[held],
        compiler_params=PARAMS,
        cost_estimate=cost(6),
        name="third_outer",
    )(square_z, w_high0, w_low0, total0)
    return pl.pallas_call(
        finish,
        out_shape=shape(2 * HALF, SLOTS, COLS, B),
        in_specs=[VMEM] * 8,
        out_specs=VMEM,
        scratch_shapes=[pltpu.VMEM((PAIRS, VIEW, 2 * B), F32), held],
        compiler_params=PARAMS,
        cost_estimate=cost(6),
        name="finish",
    )(codes, square_c, square0, square1, w_high1, w_low1, total0, total1)


def solution(mesh):
    placed = (P("row", None, "col", None), P("row", None))
    return jax.shard_map(
        shards, mesh=mesh, in_specs=placed, out_specs=P("row", None, "col", None), check_vma=False
    )
```

```python
import functools

import jax
import jax.numpy as jnp
from jax import lax
from jax.experimental import pallas as pl
from jax.experimental.pallas import tpu as pltpu
from jax.sharding import PartitionSpec as P

HALF = 6
SLOTS = 13
ONES = 7
COLS = 8
B = 128
CHUNK = HALF * ONES
PAIRS = HALF // 2
VIEW = 14 * COLS
WIDE = 26 * COLS
HALO = 18 * COLS
DEPTH = 14 * B
F32 = jnp.float32
BF16 = jnp.bfloat16
AXES = ("row", "col")


def flipped(core, index, last):
    return jnp.where(core == 0, index, last - index)


def split(value):
    high = value.astype(BF16)
    return high, (value - high.astype(F32)).astype(BF16)


def row_codes(core, pattern):
    lane = lax.broadcasted_iota(jnp.int32, pattern.shape, 1)
    rank = jnp.zeros(pattern.shape, jnp.int32)
    for s in range(SLOTS - 1):
        rank = rank + jnp.where(lane > s, pattern[:, s : s + 1], 0)
    slot = flipped(core, lane, SLOTS - 1)
    rank = flipped(core, rank, ONES - 1)
    return jnp.sum(pattern * lax.shift_left(slot, 4 * rank), axis=1, keepdims=True)


def code_of(codes, core, row):
    return codes[flipped(core, row, 2 * HALF - 1), 0]


def slot_of(code, t):
    return lax.shift_right_logical(code, 4 * t) & 15


def unused_slots(code):
    held = jnp.int32(0)
    for t in range(ONES):
        held = held | lax.shift_left(jnp.int32(1), slot_of(code, t))
    rest, rank = jnp.int32(0), jnp.int32(0)
    for s in range(SLOTS):
        off = 1 - (lax.shift_right_logical(held, s) & 1)
        rest = rest | (off * lax.shift_left(jnp.int32(s), 4 * rank))
        rank = rank + off
    return rest


def prepare(pattern_far, density_far, packed, dense0, dense1, codes, pattern, density, sems):
    core = lax.rem(lax.axis_index("row"), 2)
    get_pattern = pltpu.make_async_copy(pattern_far, pattern, sems.at[0])
    get_density = pltpu.make_async_copy(density_far, density, sems.at[1])
    get_pattern.start()
    get_density.start()
    get_pattern.wait()
    codes[...] = jnp.broadcast_to(row_codes(core, pattern[...]), codes.shape)
    get_density.wait()
    for u in range(2 * HALF):
        r = flipped(core, u, 2 * HALF - 1)
        code = codes[r, 0]
        dense = (dense0, dense1)[u // HALF]
        for s in range(SLOTS):
            dense[u % HALF, s] = jnp.zeros((COLS, B), F32)
        for t in range(ONES):
            s = slot_of(code, t)
            tile = density[r, flipped(core, s, SLOTS - 1)]
            dense[u % HALF, s] = tile
            for copy in range(4):
                packed[copy, u * ONES + t] = tile


def paired(first, second):
    gap = jnp.zeros((COLS, B), F32)
    return jnp.concatenate(
        [jnp.concatenate([first, gap], axis=0), jnp.concatenate([gap, second], axis=0)], axis=1
    )


def right_operand(chunk, before, middle, after, sides):
    def other_way(ref, v):
        return jnp.concatenate([ref[HALF - 1 - v, SLOTS - 1 - s] for s in range(SLOTS)], axis=0)

    def same_way(ref, v):
        return jnp.concatenate([ref[v, s] for s in range(SLOTS)], axis=0)

    for part, ref in enumerate((before, middle, after)):
        turned = part == (0 if chunk == 0 else 2)
        take = other_way if turned else same_way
        for i in range(PAIRS):
            high, low = split(paired(take(ref, 2 * i), take(ref, 2 * i + 1)))
            sides[part * PAIRS + i, :VIEW] = high
            sides[part * PAIRS + i, VIEW:] = low


def collect_left(chunk, near, far_m, far_p, far_o, raw):
    core = lax.rem(lax.axis_index("row"), 2)
    col = lax.axis_index("col")
    y, x = col // 4, lax.rem(col, 4)

    second = jnp.where(core == 0, y, x)
    for ref, base, step in ((near, chunk * CHUNK, 0), (far_m, 0, -1), (far_p, 0, 1), (far_o, 0, 2)):
        other = lax.rem(second + step + 4, 4)
        for i in range(4):
            spot = jnp.where(core == 0, other * 4 + i, i * 4 + other)
            rows = pl.ds(pl.multiple_of(spot * COLS, COLS), COLS)
            for t in range(CHUNK):
                raw[t, rows, :] = ref[i, base + t]


def left_operand(codes, chunk, i, raw, w_high, w_low):
    core = lax.rem(lax.axis_index("row"), 2)
    nothing = jnp.zeros((B, B), BF16)
    for q in range(2):
        v = 2 * i + q
        code = code_of(codes, core, chunk * HALF + v)
        rest = unused_slots(code)
        lanes = slice(q * B, (q + 1) * B)
        corner = slice((DEPTH - B) * (1 - q), (DEPTH - B) * (1 - q) + B)
        w_high[corner, lanes] = nothing
        w_low[corner, lanes] = nothing
        for t in range(SLOTS - ONES):
            rows = pl.ds(pl.multiple_of((slot_of(rest, t) + q) * B, B), B)
            w_high[rows, lanes] = nothing
            w_low[rows, lanes] = nothing
        for t in range(ONES):
            high, low = split(raw[v * ONES + t])
            rows = pl.ds(pl.multiple_of((slot_of(code, t) + q) * B, B), B)
            w_high[rows, lanes] = high
            w_low[rows, lanes] = low


def squares(chunk, i, sides, w_high, w_low, square, halo):
    square[i] = jnp.zeros((WIDE, 2 * B), F32)
    for m in range(7):
        depth = slice(m * 2 * B, (m + 1) * 2 * B)
        whole = jnp.dot(sides[i + m], w_high[depth], preferred_element_type=F32)
        small = jnp.dot(sides[i + m, :VIEW], w_low[depth], preferred_element_type=F32)
        square[i, 2 * COLS * m : 2 * COLS * m + VIEW] += whole[:VIEW] + whole[VIEW:] + small
    if chunk == 0:
        halo[i] = square[i, :HALO]
    else:
        halo[i] = square[i, WIDE - HALO :]


def square_kernel(chunk, codes, near, far_m, far_p, far_o, before, middle, after, square, halo, *rest):
    w_high, w_low, (raw, sides) = rest[:PAIRS], rest[PAIRS : 2 * PAIRS], rest[2 * PAIRS :]
    collect_left(chunk, near, far_m, far_p, far_o, raw)
    right_operand(chunk, before, middle, after, sides)
    left_operand(codes, chunk, 0, raw, w_high[0], w_low[0])
    for i in range(PAIRS):
        if i + 1 < PAIRS:
            left_operand(codes, chunk, i + 1, raw, w_high[i + 1], w_low[i + 1])
        squares(chunk, i, sides, w_high[i], w_low[i], square, halo)


def lift(ref, held):
    for i in range(PAIRS):
        held[0, i], held[1, i] = split(ref[i])


def lift_halo(ref, held, first):
    for i in range(PAIRS):
        source = ref[PAIRS - 1 - i]
        turned = jnp.concatenate(
            [source[(HALO // COLS - 1 - j) * COLS : (HALO // COLS - j) * COLS] for j in range(HALO // COLS)], axis=0
        )
        turned = jnp.concatenate([turned[:, B:], turned[:, :B]], axis=1)
        held[0, i, first : first + HALO], held[1, i, first : first + HALO] = split(turned)


def add_products(total, held, part, w_high, w_low):
    for i in range(PAIRS):
        value = None
        for k in range(PAIRS):
            m = part * PAIRS + k - i
            if m < 0 or m > 6:
                continue
            rows = slice(2 * COLS * (6 - m), 2 * COLS * (6 - m) + VIEW)
            depth = slice(m * 2 * B, (m + 1) * 2 * B)
            high, low = held[0, k, rows], held[1, k, rows]
            term = (
                jnp.dot(high, w_high[i][depth], preferred_element_type=F32)
                + jnp.dot(low, w_high[i][depth], preferred_element_type=F32)
                + jnp.dot(high, w_low[i][depth], preferred_element_type=F32)
            )
            value = term if value is None else value + term
        total[i] += value


def third_inner(square0, *rest):
    w_high0, w_low0, (total0, held0) = rest[:PAIRS], rest[PAIRS : 2 * PAIRS], rest[2 * PAIRS :]
    lift(square0, held0)
    total0[...] = jnp.zeros_like(total0)
    add_products(total0, held0, 1, w_high0, w_low0)


def third_second(held0, square1, before, *rest):
    w_high0, w_low0, w_high1, w_low1 = [rest[k * PAIRS : (k + 1) * PAIRS] for k in range(4)]
    total0, total1, held1 = rest[4 * PAIRS :]
    lift(square1, held1)
    total0[...] = before[...]
    total1[...] = jnp.zeros_like(total1)
    add_products(total0, held1, 2, w_high0, w_low0)
    add_products(total1, held0, 0, w_high1, w_low1)
    add_products(total1, held1, 1, w_high1, w_low1)


def finish(codes, halo0, halo1, square0, square1, before0, before1, *rest):
    w_high0, w_low0, w_high1, w_low1 = [rest[k * PAIRS : (k + 1) * PAIRS] for k in range(4)]
    out, total, held0, held1, ready, sems = rest[4 * PAIRS :]
    core = lax.rem(lax.axis_index("row"), 2)

    def write(chunk, square):
        for i in range(PAIRS):
            value = 3.0 * square[i, 6 * COLS : 6 * COLS + VIEW] - 2.0 * total[i]
            for q in range(2):
                v = 2 * i + q
                spot = flipped(core, v, HALF - 1)
                rest = unused_slots(code_of(codes, core, chunk * HALF + v))
                for s in range(SLOTS):
                    tile = value[(s + q) * COLS : (s + q + 1) * COLS, q * B : (q + 1) * B]
                    ready[chunk, spot, flipped(core, s, SLOTS - 1)] = tile
                for t in range(SLOTS - ONES):
                    place = flipped(core, slot_of(rest, t), SLOTS - 1)
                    ready[chunk, spot, place] = jnp.zeros((COLS, B), F32)
        rows = pl.ds(flipped(core, chunk * HALF, HALF), HALF)
        copy = pltpu.make_async_copy(ready.at[chunk], out.at[rows], sems.at[chunk])
        copy.start()
        return copy

    lift_halo(halo0, held0, WIDE - HALO)
    total[...] = before0[...]
    add_products(total, held0, 0, w_high0, w_low0)
    first = write(0, square0)
    lift_halo(halo1, held1, 0)
    total[...] = before1[...]
    add_products(total, held1, 2, w_high1, w_low1)
    second = write(1, square1)
    first.wait()
    second.wait()


ANY = pl.BlockSpec(memory_space=pl.ANY)
HBM = pl.BlockSpec(memory_space=pltpu.HBM)
VMEM = pl.BlockSpec(memory_space=pltpu.VMEM)
PARAMS = pltpu.CompilerParams(vmem_limit_bytes=16 * 1024 * 1024)


def cost(products):
    flops = 2 * products * 3 * VIEW * 256 * 256
    return pl.CostEstimate(flops=flops, bytes_accessed=4_000_000, transcendentals=0)


def shape(*dims, dtype=F32):
    return jax.ShapeDtypeStruct(dims, dtype)


def shards(density, pattern):
    spots = [(z, c, y, x) for z in range(16) for c in range(2) for y in range(4) for x in range(4)]

    def number(z, c, y, x):
        return (z % 16 * 2 + c) * 16 + y % 4 * 4 + x % 4

    def send(value, move):
        return lax.ppermute(value, AXES, [(number(*spot), number(*move(*spot))) for spot in spots])

    def second_way(step):
        return lambda z, c, y, x: (z, c, y + step, x) if c == 0 else (z, c, y, x + step)

    def next_chip(z, c, y, x):
        return (z - 1, 1, y, x) if c == 0 else (z + 1, 0, y, x)

    def other_core(z, c, y, x):
        return (z, 1 - c, y, x)

    dense_shape = shape(HALF, SLOTS, COLS, B)
    packed, dense0, dense1, codes = pl.pallas_call(
        prepare,
        out_shape=(shape(4, 2 * CHUNK, COLS, B), dense_shape, dense_shape, shape(2 * HALF, B, dtype=jnp.int32)),
        in_specs=[HBM, HBM],
        out_specs=(VMEM,) * 4,
        scratch_shapes=[
            pltpu.VMEM(pattern.shape, jnp.int32),
            pltpu.VMEM(density.shape, F32),
            pltpu.SemaphoreType.DMA((2,)),
        ],
        compiler_params=PARAMS,
        name="prepare",
    )(
        pltpu.with_memory_space_constraint(pattern, pltpu.HBM),
        pltpu.with_memory_space_constraint(density, pltpu.HBM),
    )

    quads = []
    for z in range(16):
        for i in range(4):
            quads.append([number(z, 0, i, x) for x in range(4)])
            quads.append([number(z, 1, y, i) for y in range(4)])
    near = lax.all_to_all(packed, AXES, 0, 0, axis_index_groups=quads)
    far = []
    for chunk in range(2):
        part = near[:, chunk * CHUNK : (chunk + 1) * CHUNK]
        far.append([send(part, second_way(step)) for step in (1, -1, 2)])
    halo_z = send(dense0, next_chip)
    weights = (shape(DEPTH, 2 * B, dtype=BF16),) * (2 * PAIRS)

    def squared(chunk, *sides):
        return pl.pallas_call(
            functools.partial(square_kernel, chunk),
            out_shape=(shape(PAIRS, WIDE, 2 * B), shape(PAIRS, HALO, 2 * B), *weights),
            in_specs=[VMEM] * 8,
            out_specs=(VMEM,) * (2 + 2 * PAIRS),
            scratch_shapes=[pltpu.VMEM((CHUNK, B, B), F32), pltpu.VMEM((3 * PAIRS, 2 * VIEW, 2 * B), BF16)],
            compiler_params=PARAMS,
            cost_estimate=cost(21),
            name=f"square{chunk}",
        )(codes, near, *far[chunk], *sides)

    square0, edge0, *w0 = squared(0, halo_z, dense0, dense1)
    square_z = send(edge0, next_chip)
    totals = shape(PAIRS, VIEW, 2 * B)
    held_shape = (2, PAIRS, WIDE, 2 * B)
    held = pltpu.VMEM(held_shape, BF16)
    total0, held0 = pl.pallas_call(
        third_inner,
        out_shape=(totals, shape(*held_shape, dtype=BF16)),
        in_specs=[VMEM] * (1 + 2 * PAIRS),
        out_specs=(VMEM, VMEM),
        compiler_params=PARAMS,
        cost_estimate=cost(9),
        name="third_inner",
    )(square0, *w0)
    dense1_later, far[1][2] = lax.optimization_barrier((dense1, far[1][2]))
    halo_c = send(dense1_later, other_core)
    halo_c, held0 = lax.optimization_barrier((halo_c, held0))
    square1, edge1, *w1 = squared(1, dense0, dense1, halo_c)
    square_c = send(edge1, other_core)
    total0, total1 = pl.pallas_call(
        third_second,
        out_shape=(totals, totals),
        in_specs=[VMEM] * (3 + 4 * PAIRS),
        out_specs=(VMEM, VMEM),
        scratch_shapes=[held],
        compiler_params=PARAMS,
        cost_estimate=cost(21),
        name="third_second",
    )(held0, square1, total0, *w0, *w1)
    return pl.pallas_call(
        finish,
        out_shape=shape(2 * HALF, SLOTS, COLS, B),
        in_specs=[VMEM] * (7 + 4 * PAIRS),
        out_specs=ANY,
        scratch_shapes=[
            pltpu.VMEM((PAIRS, VIEW, 2 * B), F32),
            held,
            held,
            pltpu.VMEM((2, HALF, SLOTS, COLS, B), F32),
            pltpu.SemaphoreType.DMA((2,)),
        ],
        compiler_params=PARAMS,
        cost_estimate=cost(12),
        name="finish",
    )(codes, square_z, square_c, square0, square1, total0, total1, *w0, *w1)


def solution(mesh):
    placed = (P("row", None, "col", None), P("row", None))
    return jax.shard_map(
        shards, mesh=mesh, in_specs=placed, out_specs=P("row", None, "col", None), check_vma=False
    )
```

```python
import functools

import jax
import jax.numpy as jnp
from jax import lax
from jax.experimental import pallas as pl
from jax.experimental.pallas import tpu as pltpu
from jax.sharding import PartitionSpec as P

HALF = 6
SLOTS = 13
ONES = 7
COLS = 8
B = 128
CHUNK = HALF * ONES
PAIRS = HALF // 2
VIEW = 14 * COLS
WIDE = 26 * COLS
HALO = 48 * COLS
DEPTH = 14 * B
F32 = jnp.float32
BF16 = jnp.bfloat16
AXES = ("row", "col")


def flipped(core, index, last):
    return jnp.where(core == 0, index, last - index)


def split(value):
    high = value.astype(BF16)
    return high, (value - high.astype(F32)).astype(BF16)


def row_codes(core, pattern):
    lane = lax.broadcasted_iota(jnp.int32, pattern.shape, 1)
    rank = jnp.zeros(pattern.shape, jnp.int32)
    for s in range(SLOTS - 1):
        rank = rank + jnp.where(lane > s, pattern[:, s : s + 1], 0)
    slot = flipped(core, lane, SLOTS - 1)
    rank = flipped(core, rank, ONES - 1)
    return jnp.sum(pattern * lax.shift_left(slot, 4 * rank), axis=1, keepdims=True)


def code_of(codes, core, row):
    return codes[flipped(core, row, 2 * HALF - 1), 0]


def slot_of(code, t):
    return lax.shift_right_logical(code, 4 * t) & 15


def unused_slots(code):
    held = jnp.int32(0)
    for t in range(ONES):
        held = held | lax.shift_left(jnp.int32(1), slot_of(code, t))
    rest, rank = jnp.int32(0), jnp.int32(0)
    for s in range(SLOTS):
        off = 1 - (lax.shift_right_logical(held, s) & 1)
        rest = rest | (off * lax.shift_left(jnp.int32(s), 4 * rank))
        rank = rank + off
    return rest


def prepare(pattern_far, density_far, packed, dense0, dense1, codes, pattern, density, sems):
    core = lax.rem(lax.axis_index("row"), 2)
    get_pattern = pltpu.make_async_copy(pattern_far, pattern, sems.at[0])
    get_density = pltpu.make_async_copy(density_far, density, sems.at[1])
    get_pattern.start()
    get_density.start()
    get_pattern.wait()
    codes[...] = jnp.broadcast_to(row_codes(core, pattern[...]), codes.shape)
    get_density.wait()
    for u in range(2 * HALF):
        r = flipped(core, u, 2 * HALF - 1)
        code = codes[r, 0]
        dense = (dense0, dense1)[u // HALF]
        for s in range(SLOTS):
            dense[u % HALF, s] = jnp.zeros((COLS, B), F32)
        for t in range(ONES):
            s = slot_of(code, t)
            tile = density[r, flipped(core, s, SLOTS - 1)]
            dense[u % HALF, s] = tile
            for copy in range(4):
                packed[copy, u * ONES + t] = tile


def paired(first, second):
    gap = jnp.zeros((COLS, B), F32)
    return jnp.concatenate(
        [jnp.concatenate([first, gap], axis=0), jnp.concatenate([gap, second], axis=0)], axis=1
    )


def right_operand(chunk, before, middle, after, sides):
    def other_way(ref, v):
        return jnp.concatenate([ref[HALF - 1 - v, SLOTS - 1 - s] for s in range(SLOTS)], axis=0)

    def same_way(ref, v):
        return jnp.concatenate([ref[v, s] for s in range(SLOTS)], axis=0)

    for part, ref in enumerate((before, middle, after)):
        turned = part == (0 if chunk == 0 else 2)
        take = other_way if turned else same_way
        for i in range(PAIRS):
            high, low = split(paired(take(ref, 2 * i), take(ref, 2 * i + 1)))
            sides[part * PAIRS + i, :VIEW] = high
            sides[part * PAIRS + i, VIEW:] = low


def collect_left(chunk, near, far_m, far_p, far_o, raw):
    core = lax.rem(lax.axis_index("row"), 2)
    col = lax.axis_index("col")
    y, x = col // 4, lax.rem(col, 4)

    second = jnp.where(core == 0, y, x)
    for ref, base, step in ((near, chunk * CHUNK, 0), (far_m, 0, -1), (far_p, 0, 1), (far_o, 0, 2)):
        other = lax.rem(second + step + 4, 4)
        for i in range(4):
            spot = jnp.where(core == 0, other * 4 + i, i * 4 + other)
            rows = pl.ds(pl.multiple_of(spot * COLS, COLS), COLS)
            for t in range(CHUNK):
                raw[t, rows, :] = ref[i, base + t]


def left_operand(codes, chunk, i, raw, w_high, w_low):
    core = lax.rem(lax.axis_index("row"), 2)
    nothing = jnp.zeros((B, B), BF16)
    for q in range(2):
        v = 2 * i + q
        code = code_of(codes, core, chunk * HALF + v)
        rest = unused_slots(code)
        lanes = slice(q * B, (q + 1) * B)
        corner = slice((DEPTH - B) * (1 - q), (DEPTH - B) * (1 - q) + B)
        w_high[corner, lanes] = nothing
        w_low[corner, lanes] = nothing
        for t in range(SLOTS - ONES):
            rows = pl.ds(pl.multiple_of((slot_of(rest, t) + q) * B, B), B)
            w_high[rows, lanes] = nothing
            w_low[rows, lanes] = nothing
        for t in range(ONES):
            high, low = split(raw[v * ONES + t])
            rows = pl.ds(pl.multiple_of((slot_of(code, t) + q) * B, B), B)
            w_high[rows, lanes] = high
            w_low[rows, lanes] = low


def edge_of(chunk, i):
    lengths = [(18 - 2 * k) * COLS if chunk == 0 else (14 + 2 * k) * COLS for k in range(PAIRS)]
    return lengths[i], sum(lengths[:i])


def squares(chunk, i, sides, w_high, w_low, square, halo):
    square[i] = jnp.zeros((WIDE, 2 * B), F32)
    for m in range(7):
        depth = slice(m * 2 * B, (m + 1) * 2 * B)
        whole = jnp.dot(sides[i + m], w_high[depth], preferred_element_type=F32)
        small = jnp.dot(sides[i + m, :VIEW], w_low[depth], preferred_element_type=F32)
        square[i, 2 * COLS * m : 2 * COLS * m + VIEW] += whole[:VIEW] + whole[VIEW:] + small
    length, start = edge_of(chunk, i)
    first = 0 if chunk == 0 else WIDE - length
    halo[start : start + length] = square[i, first : first + length]


def square_kernel(chunk, codes, near, far_m, far_p, far_o, before, middle, after, square, halo, *rest):
    w_high, w_low, (raw, sides) = rest[:PAIRS], rest[PAIRS : 2 * PAIRS], rest[2 * PAIRS :]
    collect_left(chunk, near, far_m, far_p, far_o, raw)
    right_operand(chunk, before, middle, after, sides)
    left_operand(codes, chunk, 0, raw, w_high[0], w_low[0])
    for i in range(PAIRS):
        if i + 1 < PAIRS:
            left_operand(codes, chunk, i + 1, raw, w_high[i + 1], w_low[i + 1])
        squares(chunk, i, sides, w_high[i], w_low[i], square, halo)


def lift(ref, held):
    for i in range(PAIRS):
        held[0, i], held[1, i] = split(ref[i])


def lift_halo(ref, held, chunk):
    for i in range(PAIRS):
        length, start = edge_of(chunk, PAIRS - 1 - i)
        count = length // COLS
        source = ref[start : start + length]
        turned = jnp.concatenate([source[(count - 1 - j) * COLS : (count - j) * COLS] for j in range(count)], axis=0)
        turned = jnp.concatenate([turned[:, B:], turned[:, :B]], axis=1)
        first = WIDE - length if chunk == 0 else 0
        held[0, i, first : first + length], held[1, i, first : first + length] = split(turned)


def add_products(total, held, part, w_high, w_low):
    for i in range(PAIRS):
        value = None
        for k in range(PAIRS):
            m = part * PAIRS + k - i
            if m < 0 or m > 6:
                continue
            rows = slice(2 * COLS * (6 - m), 2 * COLS * (6 - m) + VIEW)
            depth = slice(m * 2 * B, (m + 1) * 2 * B)
            high, low = held[0, k, rows], held[1, k, rows]
            term = (
                jnp.dot(high, w_high[i][depth], preferred_element_type=F32)
                + jnp.dot(low, w_high[i][depth], preferred_element_type=F32)
                + jnp.dot(high, w_low[i][depth], preferred_element_type=F32)
            )
            value = term if value is None else value + term
        total[i] += value


def third_inner(square0, *rest):
    w_high0, w_low0, (total0, held0) = rest[:PAIRS], rest[PAIRS : 2 * PAIRS], rest[2 * PAIRS :]
    lift(square0, held0)
    total0[...] = jnp.zeros_like(total0)
    add_products(total0, held0, 1, w_high0, w_low0)


def third_second(held0, square1, before, *rest):
    w_high0, w_low0, w_high1, w_low1 = [rest[k * PAIRS : (k + 1) * PAIRS] for k in range(4)]
    total0, total1, held1 = rest[4 * PAIRS :]
    lift(square1, held1)
    total0[...] = before[...]
    total1[...] = jnp.zeros_like(total1)
    add_products(total0, held1, 2, w_high0, w_low0)
    add_products(total1, held0, 0, w_high1, w_low1)
    add_products(total1, held1, 1, w_high1, w_low1)


def finish(codes, halo0, halo1, square0, square1, before0, before1, *rest):
    w_high0, w_low0, w_high1, w_low1 = [rest[k * PAIRS : (k + 1) * PAIRS] for k in range(4)]
    out, total, held0, held1, ready, sems = rest[4 * PAIRS :]
    core = lax.rem(lax.axis_index("row"), 2)

    def write(chunk, square):
        for i in range(PAIRS):
            value = 3.0 * square[i, 6 * COLS : 6 * COLS + VIEW] - 2.0 * total[i]
            for q in range(2):
                v = 2 * i + q
                spot = flipped(core, v, HALF - 1)
                rest = unused_slots(code_of(codes, core, chunk * HALF + v))
                for s in range(SLOTS):
                    tile = value[(s + q) * COLS : (s + q + 1) * COLS, q * B : (q + 1) * B]
                    ready[chunk, spot, flipped(core, s, SLOTS - 1)] = tile
                for t in range(SLOTS - ONES):
                    place = flipped(core, slot_of(rest, t), SLOTS - 1)
                    ready[chunk, spot, place] = jnp.zeros((COLS, B), F32)
        rows = pl.ds(flipped(core, chunk * HALF, HALF), HALF)
        copy = pltpu.make_async_copy(ready.at[chunk], out.at[rows], sems.at[chunk])
        copy.start()
        return copy

    lift_halo(halo0, held0, 0)
    total[...] = before0[...]
    add_products(total, held0, 0, w_high0, w_low0)
    first = write(0, square0)
    lift_halo(halo1, held1, 1)
    total[...] = before1[...]
    add_products(total, held1, 2, w_high1, w_low1)
    second = write(1, square1)
    first.wait()
    second.wait()


ANY = pl.BlockSpec(memory_space=pl.ANY)
HBM = pl.BlockSpec(memory_space=pltpu.HBM)
VMEM = pl.BlockSpec(memory_space=pltpu.VMEM)
PARAMS = pltpu.CompilerParams(vmem_limit_bytes=16 * 1024 * 1024)


def cost(products):
    flops = 2 * products * 3 * VIEW * 256 * 256
    return pl.CostEstimate(flops=flops, bytes_accessed=4_000_000, transcendentals=0)


def shape(*dims, dtype=F32):
    return jax.ShapeDtypeStruct(dims, dtype)


def shards(density, pattern):
    spots = [(z, c, y, x) for z in range(16) for c in range(2) for y in range(4) for x in range(4)]

    def number(z, c, y, x):
        return (z % 16 * 2 + c) * 16 + y % 4 * 4 + x % 4

    def send(value, move):
        return lax.ppermute(value, AXES, [(number(*spot), number(*move(*spot))) for spot in spots])

    def second_way(step):
        return lambda z, c, y, x: (z, c, y + step, x) if c == 0 else (z, c, y, x + step)

    def next_chip(z, c, y, x):
        return (z - 1, 1, y, x) if c == 0 else (z + 1, 0, y, x)

    def other_core(z, c, y, x):
        return (z, 1 - c, y, x)

    dense_shape = shape(HALF, SLOTS, COLS, B)
    packed, dense0, dense1, codes = pl.pallas_call(
        prepare,
        out_shape=(shape(4, 2 * CHUNK, COLS, B), dense_shape, dense_shape, shape(2 * HALF, B, dtype=jnp.int32)),
        in_specs=[HBM, HBM],
        out_specs=(VMEM,) * 4,
        scratch_shapes=[
            pltpu.VMEM(pattern.shape, jnp.int32),
            pltpu.VMEM(density.shape, F32),
            pltpu.SemaphoreType.DMA((2,)),
        ],
        compiler_params=PARAMS,
        name="prepare",
    )(
        pltpu.with_memory_space_constraint(pattern, pltpu.HBM),
        pltpu.with_memory_space_constraint(density, pltpu.HBM),
    )

    quads = []
    for z in range(16):
        for i in range(4):
            quads.append([number(z, 0, i, x) for x in range(4)])
            quads.append([number(z, 1, y, i) for y in range(4)])
    near = lax.all_to_all(packed, AXES, 0, 0, axis_index_groups=quads)
    far = []
    for chunk in range(2):
        part = near[:, chunk * CHUNK : (chunk + 1) * CHUNK]
        far.append([send(part, second_way(step)) for step in (1, -1, 2)])
    halo_z = send(dense0, next_chip)
    weights = (shape(DEPTH, 2 * B, dtype=BF16),) * (2 * PAIRS)

    def squared(chunk, *sides):
        return pl.pallas_call(
            functools.partial(square_kernel, chunk),
            out_shape=(shape(PAIRS, WIDE, 2 * B), shape(HALO, 2 * B), *weights),
            in_specs=[VMEM] * 8,
            out_specs=(VMEM,) * (2 + 2 * PAIRS),
            scratch_shapes=[pltpu.VMEM((CHUNK, B, B), F32), pltpu.VMEM((3 * PAIRS, 2 * VIEW, 2 * B), BF16)],
            compiler_params=PARAMS,
            cost_estimate=cost(21),
            name=f"square{chunk}",
        )(codes, near, *far[chunk], *sides)

    square0, edge0, *w0 = squared(0, halo_z, dense0, dense1)
    square_z = send(edge0, next_chip)
    totals = shape(PAIRS, VIEW, 2 * B)
    held_shape = (2, PAIRS, WIDE, 2 * B)
    held = pltpu.VMEM(held_shape, BF16)
    total0, held0 = pl.pallas_call(
        third_inner,
        out_shape=(totals, shape(*held_shape, dtype=BF16)),
        in_specs=[VMEM] * (1 + 2 * PAIRS),
        out_specs=(VMEM, VMEM),
        compiler_params=PARAMS,
        cost_estimate=cost(9),
        name="third_inner",
    )(square0, *w0)
    dense1_later, far[1][2] = lax.optimization_barrier((dense1, far[1][2]))
    halo_c = send(dense1_later, other_core)
    halo_c, held0 = lax.optimization_barrier((halo_c, held0))
    square1, edge1, *w1 = squared(1, dense0, dense1, halo_c)
    square_c = send(edge1, other_core)
    total0, total1 = pl.pallas_call(
        third_second,
        out_shape=(totals, totals),
        in_specs=[VMEM] * (3 + 4 * PAIRS),
        out_specs=(VMEM, VMEM),
        scratch_shapes=[held],
        compiler_params=PARAMS,
        cost_estimate=cost(21),
        name="third_second",
    )(held0, square1, total0, *w0, *w1)
    return pl.pallas_call(
        finish,
        out_shape=shape(2 * HALF, SLOTS, COLS, B),
        in_specs=[VMEM] * (7 + 4 * PAIRS),
        out_specs=ANY,
        scratch_shapes=[
            pltpu.VMEM((PAIRS, VIEW, 2 * B), F32),
            held,
            held,
            pltpu.VMEM((2, HALF, SLOTS, COLS, B), F32),
            pltpu.SemaphoreType.DMA((2,)),
        ],
        compiler_params=PARAMS,
        cost_estimate=cost(12),
        name="finish",
    )(codes, square_z, square_c, square0, square1, total0, total1, *w0, *w1)


def solution(mesh):
    placed = (P("row", None, "col", None), P("row", None))
    return jax.shard_map(
        shards, mesh=mesh, in_specs=placed, out_specs=P("row", None, "col", None), check_vma=False
    )
```
